256 devices in a mesh: ckpt: 8 (over z_lo, y), tensor: 8 (over z_hi, core), ex: 4 (over x).
Axes of the slice: x: 4, y: 4, z: 8 (z_hi: 4, z_lo: 2; z = z_hi * 2 + z_lo), core: 2. Of those that a mesh axis runs over, the one named last changes fastest.
Arguments:
- x_train: bfloat16 [8, 512, 5120], P('ckpt', ('tensor', 'ex')), may hold values from -6 to 6
- dy_train: bfloat16 [8, 512, 5120], P('ckpt', ('tensor', 'ex')), may hold values from -6 to 6
- x_test: bfloat16 [8, 512, 5120], P('ckpt', ('tensor', 'ex')), may hold values from -6 to 6
- dy_test: bfloat16 [8, 512, 5120], P('ckpt', ('tensor', 'ex')), may hold values from -6 to 6
- gate_train: bfloat16 [8, 512, 13824], P('ckpt', None, ('tensor', 'ex')), may hold values from -8 to 8
- gate_test: bfloat16 [8, 512, 13824], P('ckpt', None, ('tensor', 'ex')), may hold values from -8 to 8
- w_up: bfloat16 [8, 5120, 13824], P('ckpt', None, ('tensor', 'ex')), may hold values from -0.078125 to 0.078125
- w_down: bfloat16 [8, 13824, 5120], P('ckpt', ('tensor', 'ex')), may hold values from -0.078125 to 0.078125
- proj_hidden: int32 [13824, 64], P(('tensor', 'ex')), may hold values from 0 to 1
- proj_model: int32 [5120, 64], replicated, may hold values from 0 to 1
- rates: float32 [8], P('ckpt'), may hold values from 0.25 to 4
Outputs:
- scores: float32 [4, 4], P('ex')
The draws below stay inside these ranges and needn't reach their ends.
All inputs are finite; a program needn't handle non-finite values.
Results may differ from the reference program's by a relative error of at most 0.0038.
Values may be sent and summed in bfloat16 or wider, within the bound.
No kernel may reach another device: no remote copies, remote signals or barrier semaphores. Data moves between devices by JAX's collectives and lax.ppermute only.
A program may use at most 128 MiB of HBM per device.

```python
import math
import jax
import jax.numpy as jnp
from jax import lax

D = 5120
FF = 13824
KF = 64
KD = 64
SEQ = 128
CKPTS = 8
TRAIN = 4
TEST = 4


def with_ends(result, rng, low, top_value):
    place = [jax.random.randint(jax.random.fold_in(rng, axis), (), 0, length) for axis, length in enumerate(result.shape)]
    widest = result.shape.index(max(result.shape))
    next_to = place[:widest] + [(place[widest] + 1) % result.shape[widest]] + place[widest + 1:]
    return result.at[tuple(place)].set(low).at[tuple(next_to)].set(top_value)


def steps_of(key, extent, split, low, largest):
    factor_of, own = 1.0, jax.random.fold_in(key, 6)
    for position, parts in split:
        draws = jnp.exp(jax.random.uniform(jax.random.fold_in(own, position), (parts,), jnp.float32, low / len(split), largest / len(split)))
        factor_of = factor_of * jnp.repeat(draws, extent[position] // parts).reshape([-1 if axis == position else 1 for axis in range(len(extent))])
    return factor_of


def bell_draw(rng, shape, scale, reach, split=(), kind=jnp.bfloat16):
    gain = steps_of(rng, shape, split, -0.22, 0.18) if split else 1.0
    array = jax.random.normal(rng, shape, jnp.float32) * scale * gain
    return jnp.minimum(jnp.maximum(array, -reach), reach).astype(kind)


def setup_inputs(seed: int = 0) -> dict:
    keys = jax.random.split(jax.random.key(seed), 12)
    x_train = bell_draw(keys[0], (CKPTS, TRAIN * SEQ, D), 1.0, 6.0, ((0, 8), (1, 32)))
    dy_train = bell_draw(keys[1], (CKPTS, TRAIN * SEQ, D), 1.0, 6.0, ((0, 8), (1, 32)))
    x_test = bell_draw(keys[2], (CKPTS, TEST * SEQ, D), 1.0, 6.0, ((0, 8), (1, 32)))
    dy_test = bell_draw(keys[3], (CKPTS, TEST * SEQ, D), 1.0, 6.0, ((0, 8), (1, 32)))
    gate_train = bell_draw(keys[4], (CKPTS, TRAIN * SEQ, FF), 2.0, 8.0, ((0, 8), (2, 32)))
    gate_test = bell_draw(keys[5], (CKPTS, TEST * SEQ, FF), 2.0, 8.0, ((0, 8), (2, 32)))
    w_up = bell_draw(keys[6], (CKPTS, D, FF), D ** -0.5, 0.078125, ((0, 8), (2, 32)))
    w_down = bell_draw(keys[7], (CKPTS, FF, D), D ** -0.5, 0.078125, ((0, 8), (1, 32)))
    proj_hidden = with_ends(jax.random.randint(keys[8], (FF, KF), 0, 2), jax.random.fold_in(keys[8], 1), 0, 1).astype(jnp.int32)
    proj_model = with_ends(jax.random.randint(keys[9], (D, KD), 0, 2), jax.random.fold_in(keys[9], 1), 0, 1).astype(jnp.int32)
    rates = jnp.clip(jnp.exp(math.log(4.0) - 2.7725887 * jax.random.uniform(keys[10], (CKPTS,), jnp.float32) ** steps_of(keys[10], (CKPTS,), ((0, 8),), -0.2, 0.2)), 0.25, 4.0)
    return dict(x_train=x_train, dy_train=dy_train, x_test=x_test, dy_test=dy_test, gate_train=gate_train, gate_test=gate_test, w_up=w_up, w_down=w_down, proj_hidden=proj_hidden, proj_model=proj_model, rates=rates)


def block_factors(x, dy, gate, w_up, w_down, sign_h, sign_m):
    up = jnp.dot(x, w_up, preferred_element_type=jnp.float32)
    act = jax.nn.silu(gate.astype(jnp.float32))
    hidden = (act * up).astype(jnp.bfloat16)
    grad_hidden = jnp.dot(dy, w_down.T, preferred_element_type=jnp.float32)
    grad_up = (grad_hidden * act).astype(jnp.bfloat16)
    hidden_side = jnp.concatenate([jnp.dot(hidden, sign_h, preferred_element_type=jnp.float32), jnp.dot(grad_up, sign_h, preferred_element_type=jnp.float32)], axis=1) * (FF ** -0.5)
    model_side = jnp.concatenate([jnp.dot(dy, sign_m, preferred_element_type=jnp.float32), jnp.dot(x, sign_m, preferred_element_type=jnp.float32)], axis=1) * (D ** -0.5)
    return hidden_side, model_side


def sketch_rows(hidden_side, model_side):
    left = hidden_side.reshape(-1, SEQ, 2 * KF)
    right = model_side.reshape(-1, SEQ, 2 * KD)
    down = jnp.einsum("nsk,nsl->nkl", left[:, :, :KF], right[:, :, :KD], precision=lax.Precision.HIGHEST) / SEQ
    upper = jnp.einsum("nsk,nsl->nkl", right[:, :, KD:], left[:, :, KF:], precision=lax.Precision.HIGHEST) / SEQ
    count = left.shape[0]
    return jnp.concatenate([down.reshape(count, -1), upper.reshape(count, -1)], axis=1)


def reference(x_train, dy_train, x_test, dy_test, gate_train, gate_test, w_up, w_down, proj_hidden, proj_model, rates):
    sign_h = (2 * proj_hidden - 1).astype(jnp.bfloat16)
    sign_m = (2 * proj_model - 1).astype(jnp.bfloat16)
    scores = jnp.zeros((x_train.shape[1] // SEQ, x_test.shape[1] // SEQ), jnp.float32)
    for index in range(CKPTS):
        train_h, train_m = block_factors(x_train[index], dy_train[index], gate_train[index], w_up[index], w_down[index], sign_h, sign_m)
        test_h, test_m = block_factors(x_test[index], dy_test[index], gate_test[index], w_up[index], w_down[index], sign_h, sign_m)
        train_sketch = sketch_rows(train_h, train_m)
        test_sketch = sketch_rows(test_h, test_m)
        block = jnp.dot(train_sketch, test_sketch.T, precision=lax.Precision.HIGHEST, preferred_element_type=jnp.float32)
        scores = scores + rates[index] * block
    return scores
```

```python
import jax
import jax.numpy as jnp
from jax import lax
from jax.experimental import pallas as pl
from jax.experimental.pallas import tpu as pltpu
from jax.sharding import Mesh, PartitionSpec as P

D = 5120
FF = 13824
KF = 64
KD = 64
SEQ = 128
UNITS = 432
KB = 512
STEPS = D // KB
GROUP = ("zhi", "core", "ex")
EVERY = ("ckpt", "zhi", "core", "ex")


def group_pairs(dz, dc, dx):
    pairs = []
    for z in range(4):
        for c in range(2):
            for x in range(4):
                here = (z * 2 + c) * 4 + x
                there = (((z + dz) % 4) * 2 + (c + dc) % 2) * 4 + (x + dx) % 4
                pairs.append((here, there))
    return pairs


def opposed_pairs(dz, dx):
    pairs = []
    for z in range(4):
        for c in range(2):
            sign = 1 if c == 0 else -1
            for x in range(4):
                here = (z * 2 + c) * 4 + x
                there = (((z + sign * dz) % 4) * 2 + c) * 4 + (x + sign * dx) % 4
                pairs.append((here, there))
    return pairs


def y_pairs(dy):
    return [(zl * 4 + y, zl * 4 + (y + dy) % 4) for zl in range(2) for y in range(4)]


def z_pairs(d0, d1):
    pairs = []
    for z in range(8):
        for y in range(4):
            for c in range(2):
                step = d0 if c == 0 else d1
                if step is None:
                    continue
                to = (z + step) % 8
                for x in range(4):
                    here = ((((z % 2) * 4 + y) * 4 + z // 2) * 2 + c) * 4 + x
                    there = ((((to % 2) * 4 + y) * 4 + to // 2) * 2 + c) * 4 + x
                    pairs.append((here, there))
    return pairs


def move(a, dz, dc, dx):
    return lax.ppermute(a, GROUP, group_pairs(dz, dc, dx))


def plane_kernel(last, z_ref, *refs):
    (a0, a1, a2, a3, b, wu0, wu1, wd0, wd1, sm, sh0, sh1, g0, g1), refs = refs[:14], refs[14:]
    if last:
        before, outs, refs = refs[:3], refs[3:7], refs[7:]
    else:
        outs, refs = refs[:1], refs[1:]
    up0, up1, dh0, dh1, model = refs
    step = pl.program_id(0)
    pieces = (a0, a1, a2, a3)
    x = jnp.concatenate([p[0:16, :] for p in pieces] + [p[16:32, :] for p in pieces], axis=0)
    dy = jnp.concatenate([p[32:48, :] for p in pieces] + [b[...]], axis=0)
    nt = (((1,), (1,)), ((), ()))
    f32 = jnp.float32

    @pl.when(step == 0)
    def _():
        for acc in (up0, up1, dh0, dh1, model):
            acc[...] = jnp.zeros_like(acc)

    up0[...] += jnp.dot(x, wu0[...], preferred_element_type=f32)
    up1[...] += jnp.dot(x, wu1[...], preferred_element_type=f32)
    dh0[...] += lax.dot_general(dy, wd0[...], nt, preferred_element_type=f32)
    dh1[...] += lax.dot_general(dy, wd1[...], nt, preferred_element_type=f32)
    model[...] += jnp.dot(jnp.concatenate([x, dy], axis=0), sm[...], preferred_element_type=f32)

    @pl.when(step == STEPS - 1)
    def _():
        side = jnp.zeros((2 * SEQ, 128), f32)
        for up, dh, g, sh in ((up0, dh0, g0, sh0), (up1, dh1, g1, sh1)):
            gate = g[...].astype(f32)
            act = gate / (1.0 + jnp.exp(-gate))
            hidden = (act * up[...]).astype(jnp.bfloat16)
            dup = (act * dh[...]).astype(jnp.bfloat16)
            side += jnp.dot(jnp.concatenate([hidden, dup], axis=0), sh[...], preferred_element_type=f32)
        side = side * FF ** (-0.5)
        other = model[...] * D ** (-0.5)
        low = lax.broadcasted_iota(jnp.int32, (SEQ, 128), 1) < KF
        left = jnp.where(low, side[:SEQ], other[:SEQ])
        right = jnp.where(low, other[SEQ:], side[SEQ:])
        both = jnp.dot(
            left.T, right, precision=lax.Precision.HIGHEST, preferred_element_type=f32
        ) * (1.0 / SEQ)
        sketch = jnp.where(low[:KF], both[:KF], both[KF:])
        if not last:
            outs[0][...] = sketch
            return
        z = z_ref[0]
        up0[0:KF, 0:128] = sketch
        for d in range(4):
            rows = pl.ds(pl.multiple_of(((z + d) % 4) * 16, 16), 16)
            for rel in range(4):
                source = (rel + d) % 4
                value = up0[rows, 0:128] if source == 2 else before[(0, 1, None, 2)[source]][rows, :]
                outs[d][rel, :, :] = value


def plane_sketch(z, pieces, b, wu, wd, sm, sh, gates, before=None):
    last = before is not None
    whole = lambda shape: pl.BlockSpec(shape, lambda k, z: (0,) * len(shape))
    in_specs = (
        [pl.BlockSpec((48, KB), lambda k, z: (0, k))] * 4
        + [pl.BlockSpec((64, KB), lambda k, z: (0, k))]
        + [pl.BlockSpec((KB, UNITS), lambda k, z: (k, 0))] * 2
        + [pl.BlockSpec((UNITS, KB), lambda k, z: (0, k))] * 2
        + [pl.BlockSpec((KB, 128), lambda k, z: (k, 0))]
        + [whole((UNITS, 128))] * 2
        + [whole((SEQ, UNITS))] * 2
    )
    args = list(pieces) + [b, *wu, *wd, sm, *sh, *gates]
    if last:
        in_specs += [whole((KF, 128))] * 3
        args += list(before)
        out_shape = [jax.ShapeDtypeStruct((4, 16, 128), jnp.float32)] * 4
        out_specs = [whole((4, 16, 128))] * 4
    else:
        out_shape = [jax.ShapeDtypeStruct((KF, 128), jnp.float32)]
        out_specs = [whole((KF, 128))]
    outs = pl.pallas_call(
        lambda *refs: plane_kernel(last, *refs),
        grid_spec=pltpu.PrefetchScalarGridSpec(
            num_scalar_prefetch=1,
            grid=(STEPS,),
            in_specs=in_specs,
            out_specs=out_specs,
            scratch_shapes=[pltpu.VMEM((SEQ, UNITS), jnp.float32)] * 4
            + [pltpu.VMEM((2 * SEQ, 128), jnp.float32)],
        ),
        out_shape=out_shape,
        compiler_params=pltpu.CompilerParams(vmem_limit_bytes=24 * 1024 * 1024),
        cost_estimate=pl.CostEstimate(
            flops=2 * 2 * SEQ * D * 1024, bytes_accessed=4 * UNITS * D * 2, transcendentals=0
        ),
    )(z, *args)
    return outs if last else outs[0]


def ring(a, core, dz, dx):
    above = move(a, -dz, 0, -dx)
    below = move(a, dz, 0, dx)
    onward = jnp.where(core == 0, below, above)
    across = lax.ppermute(onward, GROUP, opposed_pairs(dz, dx))
    return (a, above, across, below)


def body(
    x_train,
    dy_train,
    x_test,
    dy_test,
    gate_train,
    gate_test,
    w_up,
    w_down,
    proj_hidden,
    proj_model,
    rates,
):
    core = lax.axis_index("core")
    z = lax.axis_index("zhi")
    ex = lax.axis_index("ex")
    first = core == 0

    train = jnp.concatenate([x_train[0], dy_train[0]], axis=0)
    test = jnp.concatenate([x_test[0], dy_test[0]], axis=0)
    mine = jnp.where(first, train, test)
    came = move(jnp.where(first, test, train), 0, 1, 0)
    lower = jnp.where(first, mine, came)
    upper = jnp.where(first, came, mine)
    a = jnp.concatenate([lower[:16], upper[:16], lower[16:]], axis=0)
    b = upper[16:]

    wu = (w_up[0], move(w_up[0], 0, 1, 0))
    wd = (w_down[0], move(w_down[0], 0, 1, 0))
    sign_h = (2 * proj_hidden - 1).astype(jnp.bfloat16)
    sign_h = jnp.concatenate([sign_h, sign_h], axis=1)
    sh = (sign_h, move(sign_h, 0, 1, 0))
    sign_m = (2 * proj_model - 1).astype(jnp.bfloat16)
    sm = jnp.concatenate([sign_m, sign_m], axis=1)
    gate_mine = jnp.where(first, gate_train[0], gate_test[0])
    gate_came = move(jnp.where(first, gate_test[0], gate_train[0]), 0, 1, 0)

    def plane_gate(g, dz):
        g = g.reshape(4, 2, 4, 16, UNITS)
        g = lax.dynamic_slice_in_dim(g, (z + dz) % 4, 1, 0)[0]
        g = jnp.concatenate([g, g], axis=1)
        return lax.dynamic_slice_in_dim(g, ex, 4, 1).reshape(SEQ, UNITS)

    planes = ring(a, core, 1, 0)
    b_row = jnp.concatenate(ring(b, core, 0, 1), axis=0)
    b_planes = ring(b_row, core, 1, 0)

    index = z.astype(jnp.int32).reshape(1)
    sketches = {}
    for dz in (0, 1, 3, 2):
        pieces = ring(planes[dz], core, 0, 1)
        gates = (plane_gate(gate_mine, dz), plane_gate(gate_came, dz))
        before = (sketches[0], sketches[1], sketches[3]) if dz == 2 else None
        sketches[dz] = plane_sketch(index, pieces, b_planes[dz], wu, wd, sm, sh, gates, before)

    parts = sketches[2]
    total = (parts[0] + move(parts[2], 2, 0, 0)) + (move(parts[1], 1, 0, 0) + move(parts[3], 3, 0, 0))
    total = (total + move(total, 0, 0, 2)) + (move(total, 0, 0, 1) + move(total, 0, 0, 3))
    swapped = move(total, 0, 1, 0)
    train_sum = jnp.where(first, total, swapped)
    test_sum = jnp.where(first, swapped, total)
    row = lax.dynamic_slice_in_dim(train_sum, (ex - z) % 4, 1, 0)
    products = jnp.sum(row * test_sum, axis=(1, 2)) * rates[0]
    products = lax.dynamic_slice_in_dim(jnp.concatenate([products, products]), (4 - z) % 4, 4, 0)
    block = products.reshape(1, 4)

    ckpt = lambda v, d: lax.ppermute(v, ("ckpt",), y_pairs(d))
    block = (block + ckpt(block, 2)) + (ckpt(block, 1) + ckpt(block, 3))
    line = lambda d0, d1: lax.ppermute(block, EVERY, z_pairs(d0, d1))
    r0, r1, r2, r3 = line(4, 1), line(2, -3), line(-2, 3), line(None, -1)
    half = jnp.where(first, (block + r0) + (r1 + r2), (r0 + r1) + (r2 + r3))
    return half + move(half, 0, 1, 0)


def solution(mesh):
    fine = Mesh(mesh.devices.reshape(8, 4, 2, 4), EVERY)
    rows = GROUP
    in_specs = (
        P("ckpt", rows, None),
        P("ckpt", rows, None),
        P("ckpt", rows, None),
        P("ckpt", rows, None),
        P("ckpt", None, rows),
        P("ckpt", None, rows),
        P("ckpt", None, rows),
        P("ckpt", rows, None),
        P(rows, None),
        P(),
        P("ckpt"),
    )
    out_specs = P("ex", None)
    return jax.shard_map(body, mesh=fine, in_specs=in_specs, out_specs=out_specs, check_vma=False)
```

```python
import jax
import jax.numpy as jnp
from jax import lax
from jax.experimental import pallas as pl
from jax.experimental.pallas import tpu as pltpu
from jax.sharding import Mesh, PartitionSpec as P

D = 5120
FF = 13824
KF = 64
KD = 64
SEQ = 128
ROWS = 512
UNITS = 432
STEP = 1280
HALF = D // 2
PACKED = ROWS + 128
GROUP = ("zhi", "core", "ex")
EVERY = ("ckpt", "zhi", "core", "ex")
NT = (((1,), (1,)), ((), ()))
VM = pl.BlockSpec(memory_space=pltpu.VMEM)
SM = pl.BlockSpec(memory_space=pltpu.SMEM)
ANY = pl.BlockSpec(memory_space=pl.ANY)
FREE = pl.CostEstimate(flops=0, bytes_accessed=0, transcendentals=0)
LONG = pl.CostEstimate(flops=200_000_000_000, bytes_accessed=0, transcendentals=0)


def group_pairs(dz, dc, dx):
    pairs = []
    for z in range(4):
        for c in range(2):
            for x in range(4):
                here = (z * 2 + c) * 4 + x
                there = (((z + dz) % 4) * 2 + (c + dc) % 2) * 4 + (x + dx) % 4
                pairs.append((here, there))
    return pairs


def opposed_pairs(dz, dx):
    pairs = []
    for z in range(4):
        for c in range(2):
            sign = 1 if c == 0 else -1
            for x in range(4):
                here = (z * 2 + c) * 4 + x
                there = (((z + sign * dz) % 4) * 2 + c) * 4 + (x + sign * dx) % 4
                pairs.append((here, there))
    return pairs


def y_pairs(dy):
    return [(zl * 4 + y, zl * 4 + (y + dy) % 4) for zl in range(2) for y in range(4)]


def z_pairs(d0, d1):
    pairs = []
    for z in range(8):
        for y in range(4):
            for c in range(2):
                step = d0 if c == 0 else d1
                if step is None:
                    continue
                to = (z + step) % 8
                for x in range(4):
                    here = ((((z % 2) * 4 + y) * 4 + z // 2) * 2 + c) * 4 + x
                    there = ((((to % 2) * 4 + y) * 4 + to // 2) * 2 + c) * 4 + x
                    pairs.append((here, there))
    return pairs


def move(a, dz, dc, dx):
    return lax.ppermute(a, GROUP, group_pairs(dz, dc, dx))


def call(kernel, name, args, specs, outs, deps=(), through=(), out_specs=None, scratch=(), room=6, cost=FREE):
    outs = list(outs)
    n_in, n_out, n_dep = len(args), len(outs), len(deps)
    n_pass = len(through)

    def run(*refs):
        kernel(
            *refs[:n_in],
            *refs[n_in + n_dep + n_pass : n_in + n_dep + n_pass + n_out],
            *refs[n_in + n_dep + 2 * n_pass + n_out :],
        )

    result = pl.pallas_call(
        run,
        name=name,
        in_specs=list(specs) + [ANY] * (n_dep + n_pass),
        out_specs=list(out_specs or [VM] * n_out) + [ANY] * n_pass,
        out_shape=outs + [jax.ShapeDtypeStruct(t.shape, t.dtype) for t in through],
        input_output_aliases={n_in + n_dep + i: n_out + i for i in range(n_pass)},
        scratch_shapes=list(scratch),
        compiler_params=pltpu.CompilerParams(vmem_limit_bytes=room * 1024 * 1024),
        cost_estimate=cost,
    )(*args, *deps, *through)
    return result


def shape(rows, columns, dtype=jnp.bfloat16):
    return jax.ShapeDtypeStruct((rows, columns), dtype)


def assemble(core, mine, came):
    def kernel(core, mine, came, whole):
        def put(at, rows):
            whole[at : at + 16, :] = rows

        def fill(lower, upper):
            put(0, lower[0:16, :])
            put(16, upper[0:16, :])
            put(32, lower[16:32, :])
            put(48, upper[16:32, :])

        @pl.when(core[0] == 0)
        def _():
            fill(mine, came)

        @pl.when(core[0] != 0)
        def _():
            fill(came, mine)

    outs = [shape(64, D)]
    return call(kernel, "assemble", (core, mine, came), [SM, VM, VM], outs, cost=LONG)[0]


def pick(core, below, above, deps=()):
    def kernel(core, below, above, out):
        @pl.when(core[0] == 0)
        def _():
            out[...] = below[...]

        @pl.when(core[0] != 0)
        def _():
            out[...] = above[...]

    return call(kernel, "pick", (core, below, above), [SM, VM, VM], [shape(*below.shape)], deps)[0]


def pick_halves(core, below, above, deps=()):
    def kernel(core, below0, below1, above0, above1, out):
        @pl.when(core[0] == 0)
        def _():
            out[:, 0:HALF] = below0[...]
            out[:, HALF:D] = below1[...]

        @pl.when(core[0] != 0)
        def _():
            out[:, 0:HALF] = above0[...]
            out[:, HALF:D] = above1[...]

    return call(
        kernel, "pick_halves", (core, *below, *above), [SM] + [VM] * 4, [shape(64, D)], deps
    )[0]


def regroup(pieces, deps=(), cost=FREE, later=None):
    n, width = len(pieces), pieces[0].shape[1]
    extra = () if later is None else (later,)

    def kernel(*refs):
        out = refs[n + len(extra)]
        for j in range(n):
            out[32 * j : 32 * j + 32, :] = refs[j][0:32, :]
            out[32 * (n + j) : 32 * (n + j) + 32, :] = refs[j][32:64, :]
        if extra:
            refs[n + 2][...] = refs[n][:, HALF:]

    outs = [shape(64 * n, width)] + [shape(64, HALF)] * len(extra)
    args = list(pieces) + list(extra)
    result = call(kernel, "regroup", args, [VM] * len(args), outs, deps, cost=cost)
    return result if extra else result[0]


def first_half(a, deps):
    def kernel(*refs):
        refs[1][...] = refs[0][:, :HALF]

    return call(kernel, "first_half", (a,), [VM], [shape(64, HALF)], deps)[0]


def pack(core, gate_train, gate_test, seeds, deps):
    def kernel(core, gate_train, gate_test, seeds, out):
        @pl.when(core[0] == 0)
        def _():
            out[:, 0:ROWS] = gate_test[...]

        @pl.when(core[0] != 0)
        def _():
            out[:, 0:ROWS] = gate_train[...]

        sign = (2 * seeds[...] - 1).astype(jnp.float32)
        out[:, ROWS:] = jnp.concatenate([sign, sign], axis=0).T.astype(jnp.bfloat16)

    return call(
        kernel,
        "pack",
        (core, gate_train, gate_test, seeds),
        [SM] + [VM] * 3,
        [shape(UNITS, PACKED)],
        deps,
    )[0]


def twice(seeds, deps=()):
    def kernel(seeds, out):
        sign = (2 * seeds[...] - 1).astype(jnp.float32).astype(jnp.bfloat16)
        out[0:64, :] = sign
        out[64:128, :] = sign

    return call(kernel, "twice", (seeds,), [VM], [shape(128, seeds.shape[1])], deps)[0]


def activate(where, gate, block, other=None, deps=()):
    def kernel(where, *refs):
        out, turned = refs[-2:]
        z, x = where[0], where[1]
        if other is None:
            turned[...] = refs[0][...].astype(jnp.float32).T
        else:

            @pl.when(where[2] == 0)
            def _():
                turned[...] = refs[0][...].astype(jnp.float32).T

            @pl.when(where[2] != 0)
            def _():
                turned[...] = refs[1][...].astype(jnp.float32).T

        for zo in range(4):
            for xo in range(4):
                for c in range(2):
                    source = ((((z + zo) % 4) * 2 + c) * 4 + (x + xo) % 4) * 16
                    g = turned[pl.ds(pl.multiple_of(source, 16), 16), :]
                    row = (zo * 4 + xo) * 32 + c * 16
                    out[row : row + 16, :] = g / (1.0 + jnp.exp(-g))

    gates = (gate,) if other is None else (gate, other)
    return pl.pallas_call(
        kernel,
        name="activate",
        grid=(1,),
        in_specs=[SM]
        + [pl.BlockSpec((UNITS, ROWS), lambda k: (0, block))] * len(gates)
        + [ANY] * len(deps),
        out_specs=pl.BlockSpec((ROWS, UNITS), lambda k: (0, 0)),
        out_shape=shape(ROWS, UNITS, jnp.float32),
        scratch_shapes=[pltpu.VMEM((ROWS, UNITS), jnp.float32)],
        compiler_params=pltpu.CompilerParams(vmem_limit_bytes=10 * 1024 * 1024),
        cost_estimate=FREE,
    )(where, *gates, *deps)


def sketch_of(acts, signs, ups, dhs, model_x, model_dy):
    f32 = jnp.float32
    side = None
    for act, sign, up, dh in zip(acts, signs, ups, dhs):
        hidden = (act * up).astype(jnp.bfloat16)
        dup = (act * dh).astype(jnp.bfloat16)
        part = jnp.dot(jnp.concatenate([hidden, dup], axis=0), sign, preferred_element_type=f32)
        side = part if side is None else side + part
    side = side * FF ** (-0.5)
    low = lax.broadcasted_iota(jnp.int32, (SEQ, 128), 1) < KF
    left = jnp.where(low, side[:SEQ], model_x * D ** (-0.5))
    right = jnp.where(low, model_dy * D ** (-0.5), side[SEQ:])
    both = jnp.dot(
        left.T, right, precision=lax.Precision.HIGHEST, preferred_element_type=f32
    ) * (1.0 / SEQ)
    return jnp.where(low[:KF], both[:KF], both[KF:])


def plane_pass(planes, heads, pieces, weights, packs, sm, acts, where, before=None, deps=(), halves=False):
    f32 = jnp.float32
    rows = planes[1] * SEQ
    first, planes = planes
    steps = D // STEP
    last = before is not None

    def kernel(where, *refs):
        step = pl.program_id(0)
        count = planes + 3
        given = [ref[...] for ref in refs[:count]]
        refs = refs[count:]
        if halves:
            given = [jnp.where(step < steps // 2, g, ref[...]) for g, ref in zip(given, refs)]
            refs = refs[count:]
        heads, pieces = given[:planes], given[planes:]
        weights, refs = refs[:5], refs[5:]
        act0, act1, sign0, sign1 = refs[:4]
        refs = refs[4:]
        if last:
            before, refs = refs[:2], refs[2:]
        refs = refs[len(deps) :]
        outs, refs = (refs[:4], refs[4:]) if last else (refs[:1], refs[1:])
        sums = refs

        @pl.when(step == 0)
        def _():
            for total in sums:
                total[...] = jnp.zeros_like(total)

        def tokens(first):
            parts = []
            for j in range(planes):
                parts.append(heads[j][32 * first : 32 * first + 32, :])
                at = 32 * (planes * first + j)
                parts += [p[at : at + 32, :] for p in pieces]
            return jnp.concatenate(parts, axis=0)

        x, dy = tokens(0), tokens(1)
        for j, side in enumerate((x, x, dy, dy)):
            sums[j][...] += lax.dot_general(side, weights[j][...], NT, preferred_element_type=f32)
        sums[4][...] += lax.dot_general(
            jnp.concatenate([x, dy], axis=0), weights[4][...], NT, preferred_element_type=f32
        )

        @pl.when(step == steps - 1)
        def _():
            sketches = []
            for n in range(planes):
                at = slice(n * SEQ, (n + 1) * SEQ)
                place = slice((first + 2 * n) * SEQ, (first + 2 * n + 1) * SEQ)
                sketches.append(
                    sketch_of(
                        (act0[place, :], act1[place, :]),
                        (sign0[...], sign1[...]),
                        (sums[0][at], sums[1][at]),
                        (sums[2][at], sums[3][at]),
                        sums[4][at],
                        sums[4][rows + n * SEQ : rows + (n + 1) * SEQ],
                    )
                )
            if not last:
                for n in range(planes):
                    outs[0][n * KF : (n + 1) * KF, :] = sketches[n]
                return
            sums[4][0:KF, :] = sketches[0]
            z = where[0]
            for d in range(4):
                turn = pl.multiple_of(((z + d) % 4) * 16, 16)
                for rel in range(4):
                    n = (rel + d) % 4
                    source = (before[0], before[1], sums[4], before[1])[n]
                    outs[d][rel, :, :] = source[pl.ds(turn + (KF if n == 3 else 0), 16), :]

    fixed = lambda k, w: (0, 0)
    column = lambda k, w: (0, k)
    shapes = [(rows, UNITS)] * 4 + [(2 * rows, 128)]
    if halves:
        early = lambda k, w: (0, jnp.minimum(k, steps // 2 - 1))
        late = lambda k, w: (0, jnp.maximum(k - steps // 2, 0))
    else:
        early = column
    in_specs = [pl.BlockSpec((64, STEP), early)] * planes
    in_specs += [pl.BlockSpec((64 * planes, STEP), early)] * 3
    if halves:
        in_specs += [pl.BlockSpec((64, STEP), late)] * planes
        in_specs += [pl.BlockSpec((64 * planes, STEP), late)] * 3
    in_specs += (
        [pl.BlockSpec((UNITS, STEP), column)] * 4
        + [pl.BlockSpec((128, STEP), column)]
        + [pl.BlockSpec((ROWS, UNITS), fixed)] * 2
        + [pl.BlockSpec((UNITS, 128), lambda k, w: (0, ROWS // 128))] * 2
    )
    if halves:
        args = [a for j in range(2) for a in [h[j] for h in heads] + [p[j] for p in pieces]]
    else:
        args = list(heads) + list(pieces)
    args += list(weights) + [sm] + list(acts) + list(packs)
    if last:
        args += list(before)
        in_specs += [pl.BlockSpec((KF, 128), fixed), pl.BlockSpec((2 * KF, 128), fixed)]
        out_shape = [jax.ShapeDtypeStruct((4, 16, 128), f32)] * 4
        out_specs = [pl.BlockSpec((4, 16, 128), lambda k, w: (0, 0, 0))] * 4
    else:
        out_shape = [shape(planes * KF, 128, f32)]
        out_specs = [pl.BlockSpec((planes * KF, 128), fixed)]
    outs = pl.pallas_call(
        kernel,
        name="plane_pass",
        grid_spec=pltpu.PrefetchScalarGridSpec(
            num_scalar_prefetch=1,
            grid=(steps,),
            in_specs=in_specs + [ANY] * len(deps),
            out_specs=out_specs,
            scratch_shapes=[pltpu.VMEM(s, f32) for s in shapes],
        ),
        out_shape=out_shape,
        compiler_params=pltpu.CompilerParams(vmem_limit_bytes=24 * 1024 * 1024),
        cost_estimate=FREE,
    )(where, *args, *deps)
    return outs if last else outs[0]


def both_ways(a, dz, dx):
    return move(a, dz, 0, dx), move(a, -dz, 0, -dx)


def across(a, dz, dx):
    return lax.ppermute(a, GROUP, opposed_pairs(dz, dx))


def body(
    x_train,
    dy_train,
    x_test,
    dy_test,
    gate_train,
    gate_test,
    w_up,
    w_down,
    proj_hidden,
    proj_model,
    rates,
):
    core = lax.axis_index("core")
    z = lax.axis_index("zhi")
    ex = lax.axis_index("ex")
    first = core == 0
    core1 = core.astype(jnp.int32).reshape(1)
    where = jnp.stack([z, ex, core]).astype(jnp.int32)

    away_x = jnp.where(first, x_test[0], x_train[0])
    away_dy = jnp.where(first, dy_test[0], dy_train[0])
    away = jnp.concatenate([away_x, away_dy], axis=0)
    came = move(away, 0, 1, 0)
    mine = jnp.concatenate(
        [jnp.where(first, x_train[0], x_test[0]), jnp.where(first, dy_train[0], dy_test[0])], axis=0
    )
    own = assemble(core1, mine, came)

    own_below, own_above = both_ways(own, 0, 1)
    up_came = move(w_up[0].T, 0, 1, 0)
    down_came = move(w_down[0], 0, 1, 0)
    weights = (w_up[0].T, up_came, w_down[0], down_came)
    a0_below, a0_above = both_ways(first_half(own, (up_came,)), 1, 0)
    gates = (gate_train[0].T, gate_test[0].T)
    packed = pack(core1, *gates, proj_hidden.T, (down_came,))
    packs = (packed, move(packed, 0, 1, 0))
    own_on = pick(core1, own_below, own_above)
    own_far = across(own_on, 0, 1)
    sm = twice(proj_model.T)
    acts = (
        activate(where, gates[0], 0, gates[1], (own_on,)),
        activate(where, packs[1], 0, None, (own_on,)),
    )
    near0, own1 = regroup((a0_above, a0_below), (own_on,), LONG, own)
    a1_below, a1_above = both_ways(own1, 1, 0)
    near0_below, near0_above = both_ways(near0, 0, 1)
    a_on = pick_halves(
        core1, (a0_below, a1_below), (a0_above, a1_above), (own_far, near0, sm, acts[0], acts[1])
    )
    a_far = across(a_on, 1, 0)
    near1 = regroup((a1_above, a1_below), (a_on,))
    near1_below, near1_above = both_ways(near1, 0, 1)
    rest = (weights, packs, sm, acts, where)
    near0_on = pick(core1, near0_below, near0_above, (near1,))
    near0_far = across(near0_on, 0, 1)
    sketch0 = plane_pass((0, 1), (own,), (own_above, own_far, own_below), *rest, None, (near0_on,))
    near1_on = pick(core1, near1_below, near1_above, (sketch0, a_far))
    near1_far = across(near1_on, 0, 1)
    far_below, far_above = both_ways(a_far, 0, 1)
    far_on = pick(core1, far_below, far_above, (near1_on, near0_far, near1_far))
    far_far = across(far_on, 0, 1)
    sketch13 = plane_pass(
        (1, 2),
        ((a0_above, a1_above), (a0_below, a1_below)),
        ((near0_above, near1_above), (near0_far, near1_far), (near0_below, near1_below)),
        *rest,
        None,
        (far_on,),
        True,
    )
    parts = plane_pass(
        (2, 1), (a_far,), (far_above, far_far, far_below), *rest, (sketch0, sketch13)
    )

    total = (parts[0] + move(parts[2], 2, 0, 0)) + (move(parts[1], 1, 0, 0) + move(parts[3], 3, 0, 0))
    total = (total + move(total, 0, 0, 2)) + (move(total, 0, 0, 1) + move(total, 0, 0, 3))
    swapped = move(total, 0, 1, 0)
    train_sum = jnp.where(first, total, swapped)
    test_sum = jnp.where(first, swapped, total)
    row = lax.dynamic_slice_in_dim(train_sum, (ex - z) % 4, 1, 0)
    products = jnp.sum(row * test_sum, axis=(1, 2)) * rates[0]
    products = lax.dynamic_slice_in_dim(jnp.concatenate([products, products]), (4 - z) % 4, 4, 0)
    block = products.reshape(1, 4)

    ckpt = lambda v, d: lax.ppermute(v, ("ckpt",), y_pairs(d))
    block = (block + ckpt(block, 2)) + (ckpt(block, 1) + ckpt(block, 3))
    line = lambda d0, d1: lax.ppermute(block, EVERY, z_pairs(d0, d1))
    r0, r1, r2, r3 = line(4, 1), line(2, -3), line(-2, 3), line(None, -1)
    half = jnp.where(first, (block + r0) + (r1 + r2), (r0 + r1) + (r2 + r3))
    return half + move(half, 0, 1, 0)


def solution(mesh):
    fine = Mesh(mesh.devices.reshape(8, 4, 2, 4), EVERY)
    rows = GROUP
    in_specs = (
        P("ckpt", rows, None),
        P("ckpt", rows, None),
        P("ckpt", rows, None),
        P("ckpt", rows, None),
        P("ckpt", None, rows),
        P("ckpt", None, rows),
        P("ckpt", None, rows),
        P("ckpt", rows, None),
        P(rows, None),
        P(),
        P("ckpt"),
    )
    out_specs = P("ex", None)
    return jax.shard_map(body, mesh=fine, in_specs=in_specs, out_specs=out_specs, check_vma=False)
```

```python
import jax
import jax.numpy as jnp
from jax import lax
from jax.experimental import pallas as pl
from jax.experimental.pallas import tpu as pltpu
from jax.sharding import Mesh, PartitionSpec as P

D = 5120
FF = 13824
KF = 64
KD = 64
SEQ = 128
ROWS = 512
UNITS = 432
STEP = 1280
HALF = D // 2
PACKED = ROWS + 128
GROUP = ("zhi", "core", "ex")
EVERY = ("ckpt", "zhi", "core", "ex")
NT = (((1,), (1,)), ((), ()))
VM = pl.BlockSpec(memory_space=pltpu.VMEM)
SM = pl.BlockSpec(memory_space=pltpu.SMEM)
ANY = pl.BlockSpec(memory_space=pl.ANY)
FREE = pl.CostEstimate(flops=0, bytes_accessed=0, transcendentals=0)
LONG = pl.CostEstimate(flops=200_000_000_000, bytes_accessed=0, transcendentals=0)


def group_pairs(dz, dc, dx):
    pairs = []
    for z in range(4):
        for c in range(2):
            for x in range(4):
                here = (z * 2 + c) * 4 + x
                there = (((z + dz) % 4) * 2 + (c + dc) % 2) * 4 + (x + dx) % 4
                pairs.append((here, there))
    return pairs


def opposed_pairs(dz, dx):
    pairs = []
    for z in range(4):
        for c in range(2):
            sign = 1 if c == 0 else -1
            for x in range(4):
                here = (z * 2 + c) * 4 + x
                there = (((z + sign * dz) % 4) * 2 + c) * 4 + (x + sign * dx) % 4
                pairs.append((here, there))
    return pairs


def y_pairs(dy):
    return [(zl * 4 + y, zl * 4 + (y + dy) % 4) for zl in range(2) for y in range(4)]


def z_pairs(d0, d1):
    pairs = []
    for z in range(8):
        for y in range(4):
            for c in range(2):
                step = d0 if c == 0 else d1
                if step is None:
                    continue
                to = (z + step) % 8
                for x in range(4):
                    here = ((((z % 2) * 4 + y) * 4 + z // 2) * 2 + c) * 4 + x
                    there = ((((to % 2) * 4 + y) * 4 + to // 2) * 2 + c) * 4 + x
                    pairs.append((here, there))
    return pairs


def move(a, dz, dc, dx):
    return lax.ppermute(a, GROUP, group_pairs(dz, dc, dx))


def call(kernel, name, args, specs, outs, deps=(), through=(), out_specs=None, scratch=(), room=6, cost=FREE):
    outs = list(outs)
    n_in, n_out, n_dep = len(args), len(outs), len(deps)
    n_pass = len(through)

    def run(*refs):
        kernel(
            *refs[:n_in],
            *refs[n_in + n_dep + n_pass : n_in + n_dep + n_pass + n_out],
            *refs[n_in + n_dep + 2 * n_pass + n_out :],
        )

    result = pl.pallas_call(
        run,
        name=name,
        in_specs=list(specs) + [ANY] * (n_dep + n_pass),
        out_specs=list(out_specs or [VM] * n_out) + [ANY] * n_pass,
        out_shape=outs + [jax.ShapeDtypeStruct(t.shape, t.dtype) for t in through],
        input_output_aliases={n_in + n_dep + i: n_out + i for i in range(n_pass)},
        scratch_shapes=list(scratch),
        compiler_params=pltpu.CompilerParams(vmem_limit_bytes=room * 1024 * 1024),
        cost_estimate=cost,
    )(*args, *deps, *through)
    return result


def shape(rows, columns, dtype=jnp.bfloat16):
    return jax.ShapeDtypeStruct((rows, columns), dtype)


def assemble(core, mine, came):
    def kernel(core, mine, came, whole):
        def put(at, rows):
            whole[at : at + 16, :] = rows

        def fill(lower, upper):
            put(0, lower[0:16, :])
            put(16, upper[0:16, :])
            put(32, lower[16:32, :])
            put(48, upper[16:32, :])

        @pl.when(core[0] == 0)
        def _():
            fill(mine, came)

        @pl.when(core[0] != 0)
        def _():
            fill(came, mine)

    outs = [shape(64, D)]
    return call(kernel, "assemble", (core, mine, came), [SM, VM, VM], outs, cost=LONG)[0]


def pick(core, below, above, deps=()):
    def kernel(core, below, above, out):
        @pl.when(core[0] == 0)
        def _():
            out[...] = below[...]

        @pl.when(core[0] != 0)
        def _():
            out[...] = above[...]

    return call(kernel, "pick", (core, below, above), [SM, VM, VM], [shape(*below.shape)], deps)[0]


def regroup(pieces, deps=(), cost=FREE, later=None):
    n, width = len(pieces), pieces[0].shape[1]
    extra = () if later is None else (later,)

    def kernel(*refs):
        out = refs[n + len(extra)]
        for j in range(n):
            out[32 * j : 32 * j + 32, :] = refs[j][0:32, :]
            out[32 * (n + j) : 32 * (n + j) + 32, :] = refs[j][32:64, :]
        if extra:
            refs[n + 2][...] = refs[n][:, HALF:]

    outs = [shape(64 * n, width)] + [shape(64, HALF)] * len(extra)
    args = list(pieces) + list(extra)
    result = call(kernel, "regroup", args, [VM] * len(args), outs, deps, cost=cost)
    return result if extra else result[0]


def hand(a, deps, width=HALF):
    def kernel(*refs):
        refs[1][...] = refs[0][:, :width]

    return call(kernel, "hand", (a,), [VM], [shape(64, width)], deps)[0]


def pack(core, gate_train, gate_test, seeds, deps):
    def kernel(core, gate_train, gate_test, seeds, out):
        @pl.when(core[0] == 0)
        def _():
            out[:, 0:ROWS] = gate_test[...]

        @pl.when(core[0] != 0)
        def _():
            out[:, 0:ROWS] = gate_train[...]

        sign = (2 * seeds[...] - 1).astype(jnp.float32)
        out[:, ROWS:] = jnp.concatenate([sign, sign], axis=0).T.astype(jnp.bfloat16)

    return call(
        kernel,
        "pack",
        (core, gate_train, gate_test, seeds),
        [SM] + [VM] * 3,
        [shape(UNITS, PACKED)],
        deps,
    )[0]


def twice(seeds, deps=()):
    def kernel(seeds, out):
        sign = (2 * seeds[...] - 1).astype(jnp.float32).astype(jnp.bfloat16)
        out[0:64, :] = sign
        out[64:128, :] = sign

    return call(kernel, "twice", (seeds,), [VM], [shape(128, seeds.shape[1])], deps)[0]


def activate(where, gate, block, other=None, deps=()):
    def kernel(where, *refs):
        out, turned = refs[-2:]
        z, x = where[0], where[1]
        if other is None:
            turned[...] = refs[0][...].astype(jnp.float32).T
        else:

            @pl.when(where[2] == 0)
            def _():
                turned[...] = refs[0][...].astype(jnp.float32).T

            @pl.when(where[2] != 0)
            def _():
                turned[...] = refs[1][...].astype(jnp.float32).T

        for zo in range(4):
            for xo in range(4):
                for c in range(2):
                    source = ((((z + zo) % 4) * 2 + c) * 4 + (x + xo) % 4) * 16
                    g = turned[pl.ds(pl.multiple_of(source, 16), 16), :]
                    row = (zo * 4 + xo) * 32 + c * 16
                    out[row : row + 16, :] = g / (1.0 + jnp.exp(-g))

    gates = (gate,) if other is None else (gate, other)
    return pl.pallas_call(
        kernel,
        name="activate",
        grid=(1,),
        in_specs=[SM]
        + [pl.BlockSpec((UNITS, ROWS), lambda k: (0, block))] * len(gates)
        + [ANY] * len(deps),
        out_specs=pl.BlockSpec((ROWS, UNITS), lambda k: (0, 0)),
        out_shape=shape(ROWS, UNITS, jnp.float32),
        scratch_shapes=[pltpu.VMEM((ROWS, UNITS), jnp.float32)],
        compiler_params=pltpu.CompilerParams(vmem_limit_bytes=10 * 1024 * 1024),
        cost_estimate=FREE,
    )(where, *gates, *deps)


def sketch_of(acts, signs, ups, dhs, model_x, model_dy):
    f32 = jnp.float32
    side = None
    for act, sign, up, dh in zip(acts, signs, ups, dhs):
        hidden = (act * up).astype(jnp.bfloat16)
        dup = (act * dh).astype(jnp.bfloat16)
        part = jnp.dot(jnp.concatenate([hidden, dup], axis=0), sign, preferred_element_type=f32)
        side = part if side is None else side + part
    side = side * FF ** (-0.5)
    low = lax.broadcasted_iota(jnp.int32, (SEQ, 128), 1) < KF
    left = jnp.where(low, side[:SEQ], model_x * D ** (-0.5))
    right = jnp.where(low, model_dy * D ** (-0.5), side[SEQ:])
    both = jnp.dot(
        left.T, right, precision=lax.Precision.HIGHEST, preferred_element_type=f32
    ) * (1.0 / SEQ)
    return jnp.where(low[:KF], both[:KF], both[KF:])


def plane_pass(
    planes, heads, pieces, weights, packs, sm, acts, where, half=None, sums=None, before=None, deps=()
):
    f32 = jnp.float32
    rows = planes[1] * SEQ
    first, planes = planes
    steps = D // STEP if half is None else HALF // STEP
    skip = steps if half == 1 else 0
    last = before is not None
    ends = half != 0
    n_sums = 0 if sums is None else 5

    def kernel(where, *refs):
        step = pl.program_id(0)
        heads, refs = refs[:planes], refs[planes:]
        pieces, refs = refs[:3], refs[3:]
        weights, refs = refs[:5], refs[5:]
        so_far, refs = refs[:n_sums], refs[n_sums:]
        if ends:
            act0, act1, sign0, sign1 = refs[:4]
            refs = refs[4:]
        if last:
            before, refs = refs[:2], refs[2:]
        refs = refs[len(deps) :]
        if ends:
            outs, refs = (refs[:4], refs[4:]) if last else (refs[:1], refs[1:])
        sums = refs

        @pl.when(step == 0)
        def _():
            for j, total in enumerate(sums):
                total[...] = so_far[j][...] if so_far else jnp.zeros_like(total)

        def tokens(part):
            found = []
            for j in range(planes):
                found.append(heads[j][32 * part : 32 * part + 32, :])
                at = 32 * (planes * part + j)
                found += [p[at : at + 32, :] for p in pieces]
            return jnp.concatenate(found, axis=0)

        x, dy = tokens(0), tokens(1)
        for j, side in enumerate((x, x, dy, dy)):
            sums[j][...] += lax.dot_general(side, weights[j][...], NT, preferred_element_type=f32)
        sums[4][...] += lax.dot_general(
            jnp.concatenate([x, dy], axis=0), weights[4][...], NT, preferred_element_type=f32
        )
        if not ends:
            return

        @pl.when(step == steps - 1)
        def _():
            sketches = []
            for n in range(planes):
                at = slice(n * SEQ, (n + 1) * SEQ)
                place = slice((first + 2 * n) * SEQ, (first + 2 * n + 1) * SEQ)
                sketches.append(
                    sketch_of(
                        (act0[place, :], act1[place, :]),
                        (sign0[...], sign1[...]),
                        (sums[0][at], sums[1][at]),
                        (sums[2][at], sums[3][at]),
                        sums[4][at],
                        sums[4][rows + n * SEQ : rows + (n + 1) * SEQ],
                    )
                )
            if not last:
                for n in range(planes):
                    outs[0][n * KF : (n + 1) * KF, :] = sketches[n]
                return
            sums[4][0:KF, :] = sketches[0]
            z = where[0]
            for d in range(4):
                turn = pl.multiple_of(((z + d) % 4) * 16, 16)
                for rel in range(4):
                    n = (rel + d) % 4
                    source = (before[0], before[1], sums[4], before[1])[n]
                    outs[d][rel, :, :] = source[pl.ds(turn + (KF if n == 3 else 0), 16), :]

    fixed = lambda k, w: (0, 0)
    column = lambda k, w: (0, k)
    later = lambda k, w: (0, k + skip)
    shapes = [(rows, UNITS)] * 4 + [(2 * rows, 128)]
    in_specs = [pl.BlockSpec((64, STEP), later if h.shape[1] == D else column) for h in heads]
    in_specs += [pl.BlockSpec((64 * planes, STEP), column)] * 3
    in_specs += [pl.BlockSpec((UNITS, STEP), later)] * 4 + [pl.BlockSpec((128, STEP), later)]
    args = list(heads) + list(pieces) + list(weights) + [sm] + list(sums or ())
    in_specs += [pl.BlockSpec(s, fixed) for s in shapes[:n_sums]]
    out_shape = [shape(*s, f32) for s in shapes]
    out_specs = [pl.BlockSpec(s, fixed) for s in shapes]
    scratch = []
    if ends:
        args += list(acts) + list(packs)
        in_specs += [pl.BlockSpec((ROWS, UNITS), fixed)] * 2
        in_specs += [pl.BlockSpec((UNITS, 128), lambda k, w: (0, ROWS // 128))] * 2
        scratch = [pltpu.VMEM(s, f32) for s in shapes]
        out_shape = [shape(planes * KF, 128, f32)]
        out_specs = [pl.BlockSpec((planes * KF, 128), fixed)]
    if last:
        args += list(before)
        in_specs += [pl.BlockSpec((KF, 128), fixed)] + [pl.BlockSpec((2 * KF, 128), fixed)]
        out_shape = [jax.ShapeDtypeStruct((4, 16, 128), f32)] * 4
        out_specs = [pl.BlockSpec((4, 16, 128), lambda k, w: (0, 0, 0))] * 4
    outs = pl.pallas_call(
        kernel,
        name="plane_pass",
        grid_spec=pltpu.PrefetchScalarGridSpec(
            num_scalar_prefetch=1,
            grid=(steps,),
            in_specs=in_specs + [ANY] * len(deps),
            out_specs=out_specs,
            scratch_shapes=scratch,
        ),
        out_shape=out_shape,
        compiler_params=pltpu.CompilerParams(vmem_limit_bytes=28 * 1024 * 1024),
        cost_estimate=FREE,
    )(where, *args, *deps)
    return outs[0] if ends and not last else outs


def both_ways(a, dz, dx):
    return move(a, dz, 0, dx), move(a, -dz, 0, -dx)


def across(a, dz, dx):
    return lax.ppermute(a, GROUP, opposed_pairs(dz, dx))


def body(
    x_train,
    dy_train,
    x_test,
    dy_test,
    gate_train,
    gate_test,
    w_up,
    w_down,
    proj_hidden,
    proj_model,
    rates,
):
    core = lax.axis_index("core")
    z = lax.axis_index("zhi")
    ex = lax.axis_index("ex")
    first = core == 0
    core1 = core.astype(jnp.int32).reshape(1)
    where = jnp.stack([z, ex, core]).astype(jnp.int32)

    away_x = jnp.where(first, x_test[0], x_train[0])
    away_dy = jnp.where(first, dy_test[0], dy_train[0])
    away = jnp.concatenate([away_x, away_dy], axis=0)
    came = move(away, 0, 1, 0)
    mine = jnp.concatenate(
        [jnp.where(first, x_train[0], x_test[0]), jnp.where(first, dy_train[0], dy_test[0])], axis=0
    )
    own = assemble(core1, mine, came)

    own_below, own_above = both_ways(own, 0, 1)
    up_came = move(w_up[0].T, 0, 1, 0)
    down_came = move(w_down[0], 0, 1, 0)
    weights = (w_up[0].T, up_came, w_down[0], down_came)
    a0_below, a0_above = both_ways(hand(own, (up_came,)), 1, 0)
    gates = (gate_train[0].T, gate_test[0].T)
    packed = pack(core1, *gates, proj_hidden.T, (down_came,))
    packs = (packed, move(packed, 0, 1, 0))
    own_on = pick(core1, own_below, own_above)
    own_far = across(own_on, 0, 1)
    sm = twice(proj_model.T)
    acts = (
        activate(where, gates[0], 0, gates[1], (own_on,)),
        activate(where, packs[1], 0, None, (own_on,)),
    )
    near0, own1 = regroup((a0_above, a0_below), (own_on,), LONG, own)
    a1_below, a1_above = both_ways(own1, 1, 0)
    near0_below, near0_above = both_ways(near0, 0, 1)
    a0_on = pick(core1, a0_below, a0_above, (near0,))
    a0_far = across(a0_on, 1, 0)
    near0_on = pick(core1, near0_below, near0_above, (a0_on, own_far, sm, acts[0], acts[1]))
    near0_far = across(near0_on, 0, 1)
    near1 = regroup((a1_above, a1_below), (near0_on,))
    near1_below, near1_above = both_ways(near1, 0, 1)
    a1_on = pick(core1, a1_below, a1_above, (near1,))
    a1_far = across(a1_on, 1, 0)
    rest = (weights, packs, sm, acts, where)
    sketch0 = plane_pass((0, 1), (own,), (own_above, own_far, own_below), *rest, deps=(a1_on,))
    far0_below, far0_above = both_ways(a0_far, 0, 1)
    near1_on = pick(core1, near1_below, near1_above, (sketch0,))
    near1_far = across(near1_on, 0, 1)
    sums = plane_pass(
        (1, 2),
        (a0_above, a0_below),
        (near0_above, near0_far, near0_below),
        *rest,
        half=0,
        deps=(near1_on,),
    )
    far1 = hand(a1_far, (sums[4],))
    far1_below, far1_above = both_ways(far1, 0, 1)
    far0_on = pick(core1, far0_below, far0_above, (far1,))
    far0_far = across(far0_on, 0, 1)
    sketch13 = plane_pass(
        (1, 2),
        (a1_above, a1_below),
        (near1_above, near1_far, near1_below),
        *rest,
        half=1,
        sums=sums,
        deps=(far0_on,),
    )
    far1_on = pick(core1, far1_below, far1_above, (sketch13,))
    far1_far = across(far1_on, 0, 1)
    sums = plane_pass(
        (2, 1), (a0_far,), (far0_above, far0_far, far0_below), *rest, half=0, deps=(far1_on,)
    )
    parts = plane_pass(
        (2, 1),
        (far1,),
        (far1_above, far1_far, far1_below),
        *rest,
        half=1,
        sums=sums,
        before=(sketch0, sketch13),
    )

    total = (parts[0] + move(parts[2], 2, 0, 0)) + (move(parts[1], 1, 0, 0) + move(parts[3], 3, 0, 0))
    total = (total + move(total, 0, 0, 2)) + (move(total, 0, 0, 1) + move(total, 0, 0, 3))
    swapped = move(total, 0, 1, 0)
    train_sum = jnp.where(first, total, swapped)
    test_sum = jnp.where(first, swapped, total)
    row = lax.dynamic_slice_in_dim(train_sum, (ex - z) % 4, 1, 0)
    products = jnp.sum(row * test_sum, axis=(1, 2)) * rates[0]
    products = lax.dynamic_slice_in_dim(jnp.concatenate([products, products]), (4 - z) % 4, 4, 0)
    block = products.reshape(1, 4)

    ckpt = lambda v, d: lax.ppermute(v, ("ckpt",), y_pairs(d))
    block = (block + ckpt(block, 2)) + (ckpt(block, 1) + ckpt(block, 3))
    line = lambda d0, d1: lax.ppermute(block, EVERY, z_pairs(d0, d1))
    r0, r1, r2, r3 = line(4, 1), line(2, -3), line(-2, 3), line(None, -1)
    half = jnp.where(first, (block + r0) + (r1 + r2), (r0 + r1) + (r2 + r3))
    return half + move(half, 0, 1, 0)


def solution(mesh):
    fine = Mesh(mesh.devices.reshape(8, 4, 2, 4), EVERY)
    rows = GROUP
    in_specs = (
        P("ckpt", rows, None),
        P("ckpt", rows, None),
        P("ckpt", rows, None),
        P("ckpt", rows, None),
        P("ckpt", None, rows),
        P("ckpt", None, rows),
        P("ckpt", None, rows),
        P("ckpt", rows, None),
        P(rows, None),
        P(),
        P("ckpt"),
    )
    out_specs = P("ex", None)
    return jax.shard_map(body, mesh=fine, in_specs=in_specs, out_specs=out_specs, check_vma=False)
```

```python
import jax
import jax.numpy as jnp
from jax import lax
from jax.experimental import pallas as pl
from jax.experimental.pallas import tpu as pltpu
from jax.sharding import Mesh, PartitionSpec as P

D = 5120
FF = 13824
KF = 64
KD = 64
SEQ = 128
ROWS = 512
UNITS = 432
STEP = 512
HALF = D // 2
PACKED = ROWS + 128
GROUP = ("zhi", "core", "ex")
EVERY = ("ckpt", "zhi", "core", "ex")
NT = (((1,), (1,)), ((), ()))
VM = pl.BlockSpec(memory_space=pltpu.VMEM)
SM = pl.BlockSpec(memory_space=pltpu.SMEM)
ANY = pl.BlockSpec(memory_space=pl.ANY)
FREE = pl.CostEstimate(flops=0, bytes_accessed=0, transcendentals=0)
LONG = pl.CostEstimate(flops=200_000_000_000, bytes_accessed=0, transcendentals=0)


def group_pairs(dz, dc, dx):
    pairs = []
    for z in range(4):
        for c in range(2):
            for x in range(4):
                here = (z * 2 + c) * 4 + x
                there = (((z + dz) % 4) * 2 + (c + dc) % 2) * 4 + (x + dx) % 4
                pairs.append((here, there))
    return pairs


def opposed_pairs(dz, dx):
    pairs = []
    for z in range(4):
        for c in range(2):
            sign = 1 if c == 0 else -1
            for x in range(4):
                here = (z * 2 + c) * 4 + x
                there = (((z + sign * dz) % 4) * 2 + c) * 4 + (x + sign * dx) % 4
                pairs.append((here, there))
    return pairs


def y_pairs(dy):
    return [(zl * 4 + y, zl * 4 + (y + dy) % 4) for zl in range(2) for y in range(4)]


def z_pairs(d0, d1):
    pairs = []
    for z in range(8):
        for y in range(4):
            for c in range(2):
                step = d0 if c == 0 else d1
                if step is None:
                    continue
                to = (z + step) % 8
                for x in range(4):
                    here = ((((z % 2) * 4 + y) * 4 + z // 2) * 2 + c) * 4 + x
                    there = ((((to % 2) * 4 + y) * 4 + to // 2) * 2 + c) * 4 + x
                    pairs.append((here, there))
    return pairs


def move(a, dz, dc, dx):
    return lax.ppermute(a, GROUP, group_pairs(dz, dc, dx))


def call(kernel, name, args, specs, outs, deps=(), through=(), out_specs=None, scratch=(), room=6, cost=FREE):
    outs = list(outs)
    n_in, n_out, n_dep = len(args), len(outs), len(deps)
    n_pass = len(through)

    def run(*refs):
        kernel(
            *refs[:n_in],
            *refs[n_in + n_dep + n_pass : n_in + n_dep + n_pass + n_out],
            *refs[n_in + n_dep + 2 * n_pass + n_out :],
        )

    result = pl.pallas_call(
        run,
        name=name,
        in_specs=list(specs) + [ANY] * (n_dep + n_pass),
        out_specs=list(out_specs or [VM] * n_out) + [ANY] * n_pass,
        out_shape=outs + [jax.ShapeDtypeStruct(t.shape, t.dtype) for t in through],
        input_output_aliases={n_in + n_dep + i: n_out + i for i in range(n_pass)},
        scratch_shapes=list(scratch),
        compiler_params=pltpu.CompilerParams(vmem_limit_bytes=room * 1024 * 1024),
        cost_estimate=cost,
    )(*args, *deps, *through)
    return result


def shape(rows, columns, dtype=jnp.bfloat16):
    return jax.ShapeDtypeStruct((rows, columns), dtype)


def assemble(core, mine, came):
    def kernel(core, mine, came, whole):
        def put(at, rows):
            whole[at : at + 16, :] = rows

        def fill(lower, upper):
            put(0, lower[0:16, :])
            put(16, upper[0:16, :])
            put(32, lower[16:32, :])
            put(48, upper[16:32, :])

        @pl.when(core[0] == 0)
        def _():
            fill(mine, came)

        @pl.when(core[0] != 0)
        def _():
            fill(came, mine)

    outs = [shape(64, D)]
    return call(kernel, "assemble", (core, mine, came), [SM, VM, VM], outs, cost=LONG)[0]


def pick(core, below, above, deps=()):
    def kernel(core, below, above, out):
        @pl.loop(0, below.shape[0] // 16)
        def _(i):
            rows = pl.ds(pl.multiple_of(i * 16, 16), 16)

            @pl.when(core[0] == 0)
            def _():
                out[rows, :] = below[rows, :]

            @pl.when(core[0] != 0)
            def _():
                out[rows, :] = above[rows, :]

    return call(kernel, "pick", (core, below, above), [SM, VM, VM], [shape(*below.shape)], deps)[0]


def regroup(pieces, deps=(), cost=FREE, later=None):
    n, width = len(pieces), pieces[0].shape[1]
    extra = () if later is None else (later,)

    def kernel(*refs):
        out = refs[n + len(extra)]
        for j in range(n):
            out[32 * j : 32 * j + 32, :] = refs[j][0:32, :]
            out[32 * (n + j) : 32 * (n + j) + 32, :] = refs[j][32:64, :]
        if extra:
            refs[n + 2][...] = refs[n][:, HALF:]

    outs = [shape(64 * n, width)] + [shape(64, HALF)] * len(extra)
    args = list(pieces) + list(extra)
    result = call(kernel, "regroup", args, [VM] * len(args), outs, deps, cost=cost)
    return result if extra else result[0]


def hand(a, deps, width=HALF):
    def kernel(*refs):
        refs[1][...] = refs[0][:, :width]

    return call(kernel, "hand", (a,), [VM], [shape(64, width)], deps)[0]


def pack(core, gate_train, gate_test, seeds, deps):
    def kernel(core, gate_train, gate_test, seeds, out):
        @pl.when(core[0] == 0)
        def _():
            out[:, 0:ROWS] = gate_test[...]

        @pl.when(core[0] != 0)
        def _():
            out[:, 0:ROWS] = gate_train[...]

        sign = (2 * seeds[...] - 1).astype(jnp.float32)
        out[:, ROWS:] = jnp.concatenate([sign, sign], axis=0).T.astype(jnp.bfloat16)

    return call(
        kernel,
        "pack",
        (core, gate_train, gate_test, seeds),
        [SM] + [VM] * 3,
        [shape(UNITS, PACKED)],
        deps,
    )[0]


def twice(seeds, deps=()):
    def kernel(*refs):
        seeds, out = refs

        @pl.loop(0, 4)
        def _(i):
            at = pl.multiple_of(i * 16, 16)
            sign = (2 * seeds[pl.ds(at, 16), :] - 1).astype(jnp.float32).astype(jnp.bfloat16)
            out[pl.ds(at, 16), :] = sign
            out[pl.ds(64 + at, 16), :] = sign

    return call(kernel, "twice", (seeds,), [VM], [shape(128, seeds.shape[1])], deps)[0]


def activate(where, gate, block, other=None, deps=()):
    def kernel(where, *refs):
        out, turned = refs[-2:]
        z, x = where[0], where[1]
        if other is None:
            turned[...] = refs[0][...].astype(jnp.float32).T
        else:

            @pl.when(where[2] == 0)
            def _():
                turned[...] = refs[0][...].astype(jnp.float32).T

            @pl.when(where[2] != 0)
            def _():
                turned[...] = refs[1][...].astype(jnp.float32).T

        @pl.loop(0, 32)
        def _(i):
            source = ((((z + i // 8) % 4) * 2 + i % 2) * 4 + (x + (i // 2) % 4) % 4) * 16
            g = turned[pl.ds(pl.multiple_of(source, 16), 16), :]
            out[pl.ds(pl.multiple_of(i * 16, 16), 16), :] = g / (1.0 + jnp.exp(-g))

    gates = (gate,) if other is None else (gate, other)
    return pl.pallas_call(
        kernel,
        name="activate",
        grid=(1,),
        in_specs=[SM]
        + [pl.BlockSpec((UNITS, ROWS), lambda k: (0, block))] * len(gates)
        + [ANY] * len(deps),
        out_specs=pl.BlockSpec((ROWS, UNITS), lambda k: (0, 0)),
        out_shape=shape(ROWS, UNITS, jnp.float32),
        scratch_shapes=[pltpu.VMEM((ROWS, UNITS), jnp.float32)],
        compiler_params=pltpu.CompilerParams(vmem_limit_bytes=10 * 1024 * 1024),
        cost_estimate=FREE,
    )(where, *gates, *deps)


def sketch_of(acts, signs, ups, dhs, model_x, model_dy):
    f32 = jnp.float32
    side = None
    for act, sign, up, dh in zip(acts, signs, ups, dhs):
        hidden = (act * up).astype(jnp.bfloat16)
        dup = (act * dh).astype(jnp.bfloat16)
        part = jnp.dot(jnp.concatenate([hidden, dup], axis=0), sign, preferred_element_type=f32)
        side = part if side is None else side + part
    side = side * FF ** (-0.5)
    low = lax.broadcasted_iota(jnp.int32, (SEQ, 128), 1) < KF
    left = jnp.where(low, side[:SEQ], model_x * D ** (-0.5))
    right = jnp.where(low, model_dy * D ** (-0.5), side[SEQ:])
    both = jnp.dot(
        left.T, right, precision=lax.Precision.HIGHEST, preferred_element_type=f32
    ) * (1.0 / SEQ)
    return jnp.where(low[:KF], both[:KF], both[KF:])


def plane_pass(
    planes, heads, pieces, weights, packs, sm, acts, where, half=None, sums=None, before=None, deps=()
):
    f32 = jnp.float32
    rows = planes[1] * SEQ
    first, planes = planes
    steps = D // STEP if half is None else HALF // STEP
    skip = steps if half == 1 else 0
    last = before is not None
    ends = half != 0
    n_sums = 0 if sums is None else 5

    def kernel(where, *refs):
        step = pl.program_id(0)
        heads, refs = refs[:planes], refs[planes:]
        pieces, refs = refs[:3], refs[3:]
        weights, refs = refs[:5], refs[5:]
        so_far, refs = refs[:n_sums], refs[n_sums:]
        if ends:
            act0, act1, sign0, sign1 = refs[:4]
            refs = refs[4:]
        if last:
            before, refs = refs[:2], refs[2:]
        refs = refs[len(deps) :]
        if ends:
            outs, refs = (refs[:4], refs[4:]) if last else (refs[:1], refs[1:])
        sums = refs

        @pl.when(step == 0)
        def _():
            for j, total in enumerate(sums):
                total[...] = so_far[j][...] if so_far else jnp.zeros_like(total)

        def tokens(part):
            found = []
            for j in range(planes):
                found.append(heads[j][32 * part : 32 * part + 32, :])
                at = 32 * (planes * part + j)
                found += [p[at : at + 32, :] for p in pieces]
            return jnp.concatenate(found, axis=0)

        x, dy = tokens(0), tokens(1)
        for j, side in enumerate((x, x, dy, dy)):
            sums[j][...] += lax.dot_general(side, weights[j][...], NT, preferred_element_type=f32)
        sums[4][...] += lax.dot_general(
            jnp.concatenate([x, dy], axis=0), weights[4][...], NT, preferred_element_type=f32
        )
        if not ends:
            return

        @pl.when(step == steps - 1)
        def _():
            def sketch(n):
                at = pl.ds(pl.multiple_of(n * SEQ, SEQ), SEQ)
                place = pl.ds(pl.multiple_of((first + 2 * n) * SEQ, SEQ), SEQ)
                return sketch_of(
                    (act0[place, :], act1[place, :]),
                    (sign0[...], sign1[...]),
                    (sums[0][at], sums[1][at]),
                    (sums[2][at], sums[3][at]),
                    sums[4][at],
                    sums[4][pl.ds(pl.multiple_of(rows + n * SEQ, SEQ), SEQ)],
                )

            if planes > 1:

                @pl.loop(0, planes)
                def _(n):
                    outs[0][pl.ds(pl.multiple_of(n * KF, KF), KF), :] = sketch(n)

                return
            if not last:
                outs[0][...] = sketch(0)
                return
            sums[4][0:KF, :] = sketch(0)
            z = where[0]
            for d in range(4):
                turn = pl.multiple_of(((z + d) % 4) * 16, 16)
                for rel in range(4):
                    n = (rel + d) % 4
                    source = (before[0], before[1], sums[4], before[1])[n]
                    outs[d][rel, :, :] = source[pl.ds(turn + (KF if n == 3 else 0), 16), :]

    fixed = lambda k, w: (0, 0)
    column = lambda k, w: (0, k)
    later = lambda k, w: (0, k + skip)
    shapes = [(rows, UNITS)] * 4 + [(2 * rows, 128)]
    in_specs = [pl.BlockSpec((64, STEP), later if h.shape[1] == D else column) for h in heads]
    in_specs += [pl.BlockSpec((64 * planes, STEP), column)] * 3
    in_specs += [pl.BlockSpec((UNITS, STEP), later)] * 4 + [pl.BlockSpec((128, STEP), later)]
    args = list(heads) + list(pieces) + list(weights) + [sm] + list(sums or ())
    in_specs += [pl.BlockSpec(s, fixed) for s in shapes[:n_sums]]
    out_shape = [shape(*s, f32) for s in shapes]
    out_specs = [pl.BlockSpec(s, fixed) for s in shapes]
    scratch = []
    if ends:
        args += list(acts) + list(packs)
        in_specs += [pl.BlockSpec((ROWS, UNITS), fixed)] * 2
        in_specs += [pl.BlockSpec((UNITS, 128), lambda k, w: (0, ROWS // 128))] * 2
        scratch = [pltpu.VMEM(s, f32) for s in shapes]
        out_shape = [shape(planes * KF, 128, f32)]
        out_specs = [pl.BlockSpec((planes * KF, 128), fixed)]
    if last:
        args += list(before)
        in_specs += [pl.BlockSpec((KF, 128), fixed)] + [pl.BlockSpec((2 * KF, 128), fixed)]
        out_shape = [jax.ShapeDtypeStruct((4, 16, 128), f32)] * 4
        out_specs = [pl.BlockSpec((4, 16, 128), lambda k, w: (0, 0, 0))] * 4
    outs = pl.pallas_call(
        kernel,
        name="plane_pass",
        grid_spec=pltpu.PrefetchScalarGridSpec(
            num_scalar_prefetch=1,
            grid=(steps,),
            in_specs=in_specs + [ANY] * len(deps),
            out_specs=out_specs,
            scratch_shapes=scratch,
        ),
        out_shape=out_shape,
        compiler_params=pltpu.CompilerParams(vmem_limit_bytes=28 * 1024 * 1024),
        cost_estimate=FREE,
    )(where, *args, *deps)
    return outs[0] if ends and not last else outs


def both_ways(a, dz, dx):
    return move(a, dz, 0, dx), move(a, -dz, 0, -dx)


def across(a, dz, dx):
    return lax.ppermute(a, GROUP, opposed_pairs(dz, dx))


def body(
    x_train,
    dy_train,
    x_test,
    dy_test,
    gate_train,
    gate_test,
    w_up,
    w_down,
    proj_hidden,
    proj_model,
    rates,
):
    core = lax.axis_index("core")
    z = lax.axis_index("zhi")
    ex = lax.axis_index("ex")
    first = core == 0
    core1 = core.astype(jnp.int32).reshape(1)
    where = jnp.stack([z, ex, core]).astype(jnp.int32)

    away_x = jnp.where(first, x_test[0], x_train[0])
    away_dy = jnp.where(first, dy_test[0], dy_train[0])
    away = jnp.concatenate([away_x, away_dy], axis=0)
    came = move(away, 0, 1, 0)
    mine = jnp.concatenate(
        [jnp.where(first, x_train[0], x_test[0]), jnp.where(first, dy_train[0], dy_test[0])], axis=0
    )
    own = assemble(core1, mine, came)

    own_below, own_above = both_ways(own, 0, 1)
    up_came = move(w_up[0].T, 0, 1, 0)
    down_came = move(w_down[0], 0, 1, 0)
    weights = (w_up[0].T, up_came, w_down[0], down_came)
    a0_below, a0_above = both_ways(hand(own, (up_came,)), 1, 0)
    gates = (gate_train[0].T, gate_test[0].T)
    packed = pack(core1, *gates, proj_hidden.T, (down_came,))
    packs = (packed, move(packed, 0, 1, 0))
    own_on = pick(core1, own_below, own_above)
    own_far = across(own_on, 0, 1)
    sm = twice(proj_model.T)
    acts = (
        activate(where, gates[0], 0, gates[1], (own_on,)),
        activate(where, packs[1], 0, None, (own_on,)),
    )
    near0, own1 = regroup((a0_above, a0_below), (own_on,), LONG, own)
    a1_below, a1_above = both_ways(own1, 1, 0)
    near0_below, near0_above = both_ways(near0, 0, 1)
    a0_on = pick(core1, a0_below, a0_above, (near0,))
    a0_far = across(a0_on, 1, 0)
    near0_on = pick(core1, near0_below, near0_above, (a0_on, own_far, sm, acts[0], acts[1]))
    near0_far = across(near0_on, 0, 1)
    near1 = regroup((a1_above, a1_below), (near0_on,))
    near1_below, near1_above = both_ways(near1, 0, 1)
    a1_on = pick(core1, a1_below, a1_above, (near1,))
    a1_far = across(a1_on, 1, 0)
    rest = (weights, packs, sm, acts, where)
    sketch0 = plane_pass((0, 1), (own,), (own_above, own_far, own_below), *rest, deps=(a1_on,))
    far0_below, far0_above = both_ways(a0_far, 0, 1)
    near1_on = pick(core1, near1_below, near1_above, (sketch0,))
    near1_far = across(near1_on, 0, 1)
    sums = plane_pass(
        (1, 2),
        (a0_above, a0_below),
        (near0_above, near0_far, near0_below),
        *rest,
        half=0,
        deps=(near1_on,),
    )
    far1 = hand(a1_far, (sums[4],))
    far1_below, far1_above = both_ways(far1, 0, 1)
    far0_on = pick(core1, far0_below, far0_above, (far1,))
    far0_far = across(far0_on, 0, 1)
    sketch13 = plane_pass(
        (1, 2),
        (a1_above, a1_below),
        (near1_above, near1_far, near1_below),
        *rest,
        half=1,
        sums=sums,
        deps=(far0_on,),
    )
    far1_on = pick(core1, far1_below, far1_above, (sketch13,))
    far1_far = across(far1_on, 0, 1)
    sums = plane_pass(
        (2, 1), (a0_far,), (far0_above, far0_far, far0_below), *rest, half=0, deps=(far1_on,)
    )
    parts = plane_pass(
        (2, 1),
        (far1,),
        (far1_above, far1_far, far1_below),
        *rest,
        half=1,
        sums=sums,
        before=(sketch0, sketch13),
    )

    total = (parts[0] + move(parts[2], 2, 0, 0)) + (move(parts[1], 1, 0, 0) + move(parts[3], 3, 0, 0))
    total = (total + move(total, 0, 0, 2)) + (move(total, 0, 0, 1) + move(total, 0, 0, 3))
    swapped = move(total, 0, 1, 0)
    train_sum = jnp.where(first, total, swapped)
    test_sum = jnp.where(first, swapped, total)
    row = lax.dynamic_slice_in_dim(train_sum, (ex - z) % 4, 1, 0)
    products = jnp.sum(row * test_sum, axis=(1, 2)) * rates[0]
    products = lax.dynamic_slice_in_dim(jnp.concatenate([products, products]), (4 - z) % 4, 4, 0)
    block = products.reshape(1, 4)

    ckpt = lambda v, d: lax.ppermute(v, ("ckpt",), y_pairs(d))
    block = (block + ckpt(block, 2)) + (ckpt(block, 1) + ckpt(block, 3))
    line = lambda d0, d1: lax.ppermute(block, EVERY, z_pairs(d0, d1))
    r0, r1, r2, r3 = line(4, 1), line(2, -3), line(-2, 3), line(None, -1)
    half = jnp.where(first, (block + r0) + (r1 + r2), (r0 + r1) + (r2 + r3))
    return half + move(half, 0, 1, 0)


def solution(mesh):
    fine = Mesh(mesh.devices.reshape(8, 4, 2, 4), EVERY)
    rows = GROUP
    in_specs = (
        P("ckpt", rows, None),
        P("ckpt", rows, None),
        P("ckpt", rows, None),
        P("ckpt", rows, None),
        P("ckpt", None, rows),
        P("ckpt", None, rows),
        P("ckpt", None, rows),
        P("ckpt", rows, None),
        P(rows, None),
        P(),
        P("ckpt"),
    )
    out_specs = P("ex", None)
    return jax.shard_map(body, mesh=fine, in_specs=in_specs, out_specs=out_specs, check_vma=False)
```

```python
import jax
import jax.numpy as jnp
from jax import lax
from jax.experimental import pallas as pl
from jax.experimental.pallas import tpu as pltpu
from jax.sharding import Mesh, PartitionSpec as P

D = 5120
FF = 13824
KF = 64
KD = 64
SEQ = 128
ROWS = 512
UNITS = 432
HALF = D // 2
PACKED = ROWS + 128
GROUP = ("zhi", "core", "ex")
EVERY = ("ckpt", "zhi", "core", "ex")
NT = (((1,), (1,)), ((), ()))
VM = pl.BlockSpec(memory_space=pltpu.VMEM)
SM = pl.BlockSpec(memory_space=pltpu.SMEM)
ANY = pl.BlockSpec(memory_space=pl.ANY)
FREE = pl.CostEstimate(flops=0, bytes_accessed=0, transcendentals=0)
LONG = pl.CostEstimate(flops=200_000_000_000, bytes_accessed=0, transcendentals=0)


def group_pairs(dz, dc, dx):
    pairs = []
    for z in range(4):
        for c in range(2):
            for x in range(4):
                here = (z * 2 + c) * 4 + x
                there = (((z + dz) % 4) * 2 + (c + dc) % 2) * 4 + (x + dx) % 4
                pairs.append((here, there))
    return pairs


def opposed_pairs(dz, dx):
    pairs = []
    for z in range(4):
        for c in range(2):
            sign = 1 if c == 0 else -1
            for x in range(4):
                here = (z * 2 + c) * 4 + x
                there = (((z + sign * dz) % 4) * 2 + c) * 4 + (x + sign * dx) % 4
                pairs.append((here, there))
    return pairs


def y_pairs(dy):
    return [(zl * 4 + y, zl * 4 + (y + dy) % 4) for zl in range(2) for y in range(4)]


def z_pairs(d0, d1):
    pairs = []
    for z in range(8):
        for y in range(4):
            for c in range(2):
                step = d0 if c == 0 else d1
                if step is None:
                    continue
                to = (z + step) % 8
                for x in range(4):
                    here = ((((z % 2) * 4 + y) * 4 + z // 2) * 2 + c) * 4 + x
                    there = ((((to % 2) * 4 + y) * 4 + to // 2) * 2 + c) * 4 + x
                    pairs.append((here, there))
    return pairs


def move(a, dz, dc, dx):
    return lax.ppermute(a, GROUP, group_pairs(dz, dc, dx))


def call(kernel, name, args, specs, outs, deps=(), through=(), out_specs=None, scratch=(), room=6, cost=FREE):
    outs = list(outs)
    n_in, n_out, n_dep = len(args), len(outs), len(deps)
    n_pass = len(through)

    def run(*refs):
        kernel(
            *refs[:n_in],
            *refs[n_in + n_dep + n_pass : n_in + n_dep + n_pass + n_out],
            *refs[n_in + n_dep + 2 * n_pass + n_out :],
        )

    result = pl.pallas_call(
        run,
        name=name,
        in_specs=list(specs) + [ANY] * (n_dep + n_pass),
        out_specs=list(out_specs or [VM] * n_out) + [ANY] * n_pass,
        out_shape=outs + [jax.ShapeDtypeStruct(t.shape, t.dtype) for t in through],
        input_output_aliases={n_in + n_dep + i: n_out + i for i in range(n_pass)},
        scratch_shapes=list(scratch),
        compiler_params=pltpu.CompilerParams(vmem_limit_bytes=room * 1024 * 1024),
        cost_estimate=cost,
    )(*args, *deps, *through)
    return result


def shape(rows, columns, dtype=jnp.bfloat16):
    return jax.ShapeDtypeStruct((rows, columns), dtype)


def assemble(core, mine, came):
    def kernel(core, mine, came, whole):
        def put(at, rows):
            whole[at : at + 16, :] = rows

        def fill(lower, upper):
            put(0, lower[0:16, :])
            put(16, upper[0:16, :])
            put(32, lower[16:32, :])
            put(48, upper[16:32, :])

        @pl.when(core[0] == 0)
        def _():
            fill(mine, came)

        @pl.when(core[0] != 0)
        def _():
            fill(came, mine)

    outs = [shape(64, D)]
    return call(kernel, "assemble", (core, mine, came), [SM, VM, VM], outs, cost=LONG)[0]


def pick(core, below, above, deps=()):
    def kernel(core, below, above, out):
        @pl.loop(0, below.shape[0] // 16)
        def _(i):
            rows = pl.ds(pl.multiple_of(i * 16, 16), 16)

            @pl.when(core[0] == 0)
            def _():
                out[rows, :] = below[rows, :]

            @pl.when(core[0] != 0)
            def _():
                out[rows, :] = above[rows, :]

    return call(kernel, "pick", (core, below, above), [SM, VM, VM], [shape(*below.shape)], deps)[0]


def regroup(pieces, deps=(), cost=FREE, later=None):
    n, width = len(pieces), pieces[0].shape[1]
    extra = () if later is None else (later,)

    def kernel(*refs):
        out = refs[n + len(extra)]
        for j in range(n):
            out[32 * j : 32 * j + 32, :] = refs[j][0:32, :]
            out[32 * (n + j) : 32 * (n + j) + 32, :] = refs[j][32:64, :]
        if extra:
            refs[n + 2][...] = refs[n][:, HALF:]

    outs = [shape(64 * n, width)] + [shape(64, HALF)] * len(extra)
    args = list(pieces) + list(extra)
    result = call(kernel, "regroup", args, [VM] * len(args), outs, deps, cost=cost)
    return result if extra else result[0]


def hand(a, deps, width=HALF):
    def kernel(*refs):
        refs[1][...] = refs[0][:, :width]

    return call(kernel, "hand", (a,), [VM], [shape(64, width)], deps)[0]


def pack(core, gate_train, gate_test, seeds, deps):
    def kernel(core, gate_train, gate_test, seeds, out):
        @pl.when(core[0] == 0)
        def _():
            out[:, 0:ROWS] = gate_test[...]

        @pl.when(core[0] != 0)
        def _():
            out[:, 0:ROWS] = gate_train[...]

        sign = (2 * seeds[...] - 1).astype(jnp.float32)
        out[:, ROWS:] = jnp.concatenate([sign, sign], axis=0).T.astype(jnp.bfloat16)

    return call(
        kernel,
        "pack",
        (core, gate_train, gate_test, seeds),
        [SM] + [VM] * 3,
        [shape(UNITS, PACKED)],
        deps,
    )[0]


def twice(seeds, deps=()):
    def kernel(*refs):
        seeds, out = refs

        @pl.loop(0, 4)
        def _(i):
            at = pl.multiple_of(i * 16, 16)
            sign = (2 * seeds[pl.ds(at, 16), :] - 1).astype(jnp.float32).astype(jnp.bfloat16)
            out[pl.ds(at, 16), :] = sign
            out[pl.ds(64 + at, 16), :] = sign

    return call(kernel, "twice", (seeds,), [VM], [shape(128, seeds.shape[1])], deps)[0]


def activate(where, gate, block, other=None, deps=()):
    def kernel(where, *refs):
        out, turned = refs[-2:]
        z, x = where[0], where[1]
        if other is None:
            turned[...] = refs[0][...].astype(jnp.float32).T
        else:

            @pl.when(where[2] == 0)
            def _():
                turned[...] = refs[0][...].astype(jnp.float32).T

            @pl.when(where[2] != 0)
            def _():
                turned[...] = refs[1][...].astype(jnp.float32).T

        @pl.loop(0, 32)
        def _(i):
            source = ((((z + i // 8) % 4) * 2 + i % 2) * 4 + (x + (i // 2) % 4) % 4) * 16
            g = turned[pl.ds(pl.multiple_of(source, 16), 16), :]
            out[pl.ds(pl.multiple_of(i * 16, 16), 16), :] = g / (1.0 + jnp.exp(-g))

    gates = (gate,) if other is None else (gate, other)
    return pl.pallas_call(
        kernel,
        name="activate",
        grid=(1,),
        in_specs=[SM]
        + [pl.BlockSpec((UNITS, ROWS), lambda k: (0, block))] * len(gates)
        + [ANY] * len(deps),
        out_specs=pl.BlockSpec((ROWS, UNITS), lambda k: (0, 0)),
        out_shape=shape(ROWS, UNITS, jnp.float32),
        scratch_shapes=[pltpu.VMEM((ROWS, UNITS), jnp.float32)],
        compiler_params=pltpu.CompilerParams(vmem_limit_bytes=10 * 1024 * 1024),
        cost_estimate=FREE,
    )(where, *gates, *deps)


def sketch_of(acts, signs, ups, dhs, model_x, model_dy):
    f32 = jnp.float32
    side = None
    for act, sign, up, dh in zip(acts, signs, ups, dhs):
        hidden = (act * up).astype(jnp.bfloat16)
        dup = (act * dh).astype(jnp.bfloat16)
        part = jnp.dot(jnp.concatenate([hidden, dup], axis=0), sign, preferred_element_type=f32)
        side = part if side is None else side + part
    side = side * FF ** (-0.5)
    low = lax.broadcasted_iota(jnp.int32, (SEQ, 128), 1) < KF
    left = jnp.where(low, side[:SEQ], model_x * D ** (-0.5))
    right = jnp.where(low, model_dy * D ** (-0.5), side[SEQ:])
    both = jnp.dot(
        left.T, right, precision=lax.Precision.HIGHEST, preferred_element_type=f32
    ) * (1.0 / SEQ)
    return jnp.where(low[:KF], both[:KF], both[KF:])


def plane_pass(
    planes, heads, pieces, weights, packs, sm, acts, where, half=None, sums=None, before=None, deps=()
):
    f32 = jnp.float32
    rows = planes[1] * SEQ
    first, planes = planes
    last = before is not None
    width = 1280 if last else 512
    steps = D // width if half is None else HALF // width
    skip = steps if half == 1 else 0
    ends = half != 0
    n_sums = 0 if sums is None else 5

    def kernel(where, *refs):
        step = pl.program_id(0)
        heads, refs = refs[:planes], refs[planes:]
        pieces, refs = refs[:3], refs[3:]
        weights, refs = refs[:5], refs[5:]
        so_far, refs = refs[:n_sums], refs[n_sums:]
        if ends:
            act0, act1, sign0, sign1 = refs[:4]
            refs = refs[4:]
        if last:
            before, refs = refs[:2], refs[2:]
        refs = refs[len(deps) :]
        if ends:
            outs, refs = (refs[:4], refs[4:]) if last else (refs[:1], refs[1:])
        sums = refs

        @pl.when(step == 0)
        def _():
            for j, total in enumerate(sums):
                total[...] = so_far[j][...] if so_far else jnp.zeros_like(total)

        def tokens(part):
            found = []
            for j in range(planes):
                found.append(heads[j][32 * part : 32 * part + 32, :])
                at = 32 * (planes * part + j)
                found += [p[at : at + 32, :] for p in pieces]
            return jnp.concatenate(found, axis=0)

        x, dy = tokens(0), tokens(1)
        for j, side in enumerate((x, x, dy, dy)):
            sums[j][...] += lax.dot_general(side, weights[j][...], NT, preferred_element_type=f32)
        sums[4][...] += lax.dot_general(
            jnp.concatenate([x, dy], axis=0), weights[4][...], NT, preferred_element_type=f32
        )
        if not ends:
            return

        @pl.when(step == steps - 1)
        def _():
            def sketch(n):
                at = pl.ds(pl.multiple_of(n * SEQ, SEQ), SEQ)
                place = pl.ds(pl.multiple_of((first + 2 * n) * SEQ, SEQ), SEQ)
                return sketch_of(
                    (act0[place, :], act1[place, :]),
                    (sign0[...], sign1[...]),
                    (sums[0][at], sums[1][at]),
                    (sums[2][at], sums[3][at]),
                    sums[4][at],
                    sums[4][pl.ds(pl.multiple_of(rows + n * SEQ, SEQ), SEQ)],
                )

            if planes > 1:

                @pl.loop(0, planes)
                def _(n):
                    outs[0][pl.ds(pl.multiple_of(n * KF, KF), KF), :] = sketch(n)

                return
            if not last:
                outs[0][...] = sketch(0)
                return
            sums[4][0:KF, :] = sketch(0)
            z = where[0]
            for d in range(4):
                turn = pl.multiple_of(((z + d) % 4) * 16, 16)
                for rel in range(4):
                    n = (rel + d) % 4
                    source = (before[0], before[1], sums[4], before[1])[n]
                    outs[d][rel, :, :] = source[pl.ds(turn + (KF if n == 3 else 0), 16), :]

    fixed = lambda k, w: (0, 0)
    column = lambda k, w: (0, k)
    later = lambda k, w: (0, k + skip)
    shapes = [(rows, UNITS)] * 4 + [(2 * rows, 128)]
    in_specs = [pl.BlockSpec((64, width), later if h.shape[1] == D else column) for h in heads]
    in_specs += [pl.BlockSpec((64 * planes, width), column)] * 3
    in_specs += [pl.BlockSpec((UNITS, width), later)] * 4 + [pl.BlockSpec((128, width), later)]
    args = list(heads) + list(pieces) + list(weights) + [sm] + list(sums or ())
    in_specs += [pl.BlockSpec(s, fixed) for s in shapes[:n_sums]]
    out_shape = [shape(*s, f32) for s in shapes]
    out_specs = [pl.BlockSpec(s, fixed) for s in shapes]
    scratch = []
    if ends:
        args += list(acts) + list(packs)
        in_specs += [pl.BlockSpec((ROWS, UNITS), fixed)] * 2
        in_specs += [pl.BlockSpec((UNITS, 128), lambda k, w: (0, ROWS // 128))] * 2
        scratch = [pltpu.VMEM(s, f32) for s in shapes]
        out_shape = [shape(planes * KF, 128, f32)]
        out_specs = [pl.BlockSpec((planes * KF, 128), fixed)]
    if last:
        args += list(before)
        in_specs += [pl.BlockSpec((KF, 128), fixed)] + [pl.BlockSpec((2 * KF, 128), fixed)]
        out_shape = [jax.ShapeDtypeStruct((4, 16, 128), f32)] * 4
        out_specs = [pl.BlockSpec((4, 16, 128), lambda k, w: (0, 0, 0))] * 4
    outs = pl.pallas_call(
        kernel,
        name="plane_pass",
        grid_spec=pltpu.PrefetchScalarGridSpec(
            num_scalar_prefetch=1,
            grid=(steps,),
            in_specs=in_specs + [ANY] * len(deps),
            out_specs=out_specs,
            scratch_shapes=scratch,
        ),
        out_shape=out_shape,
        compiler_params=pltpu.CompilerParams(vmem_limit_bytes=28 * 1024 * 1024),
        cost_estimate=FREE,
    )(where, *args, *deps)
    return outs[0] if ends and not last else outs


def both_ways(a, dz, dx):
    return move(a, dz, 0, dx), move(a, -dz, 0, -dx)


def across(a, dz, dx):
    return lax.ppermute(a, GROUP, opposed_pairs(dz, dx))


def body(
    x_train,
    dy_train,
    x_test,
    dy_test,
    gate_train,
    gate_test,
    w_up,
    w_down,
    proj_hidden,
    proj_model,
    rates,
):
    core = lax.axis_index("core")
    z = lax.axis_index("zhi")
    ex = lax.axis_index("ex")
    first = core == 0
    core1 = core.astype(jnp.int32).reshape(1)
    where = jnp.stack([z, ex, core]).astype(jnp.int32)

    away_x = jnp.where(first, x_test[0], x_train[0])
    away_dy = jnp.where(first, dy_test[0], dy_train[0])
    away = jnp.concatenate([away_x, away_dy], axis=0)
    came = move(away, 0, 1, 0)
    mine = jnp.concatenate(
        [jnp.where(first, x_train[0], x_test[0]), jnp.where(first, dy_train[0], dy_test[0])], axis=0
    )
    own = assemble(core1, mine, came)

    own_below, own_above = both_ways(own, 0, 1)
    up_came = move(w_up[0].T, 0, 1, 0)
    down_came = move(w_down[0], 0, 1, 0)
    weights = (w_up[0].T, up_came, w_down[0], down_came)
    a0_below, a0_above = both_ways(hand(own, (up_came,)), 1, 0)
    gates = (gate_train[0].T, gate_test[0].T)
    packed = pack(core1, *gates, proj_hidden.T, (down_came,))
    packs = (packed, move(packed, 0, 1, 0))
    own_on = pick(core1, own_below, own_above)
    own_far = across(own_on, 0, 1)
    sm = twice(proj_model.T)
    acts = (
        activate(where, gates[0], 0, gates[1], (own_on,)),
        activate(where, packs[1], 0, None, (own_on,)),
    )
    near0, own1 = regroup((a0_above, a0_below), (own_on,), LONG, own)
    a1_below, a1_above = both_ways(own1, 1, 0)
    near0_below, near0_above = both_ways(near0, 0, 1)
    a0_on = pick(core1, a0_below, a0_above, (near0,))
    a0_far = across(a0_on, 1, 0)
    near0_on = pick(core1, near0_below, near0_above, (a0_on, own_far, sm, acts[0], acts[1]))
    near0_far = across(near0_on, 0, 1)
    near1 = regroup((a1_above, a1_below), (near0_on,))
    near1_below, near1_above = both_ways(near1, 0, 1)
    a1_on = pick(core1, a1_below, a1_above, (near1,))
    a1_far = across(a1_on, 1, 0)
    rest = (weights, packs, sm, acts, where)
    sketch0 = plane_pass((0, 1), (own,), (own_above, own_far, own_below), *rest, deps=(a1_on,))
    far0_below, far0_above = both_ways(a0_far, 0, 1)
    near1_on = pick(core1, near1_below, near1_above, (sketch0,))
    near1_far = across(near1_on, 0, 1)
    sums = plane_pass(
        (1, 2),
        (a0_above, a0_below),
        (near0_above, near0_far, near0_below),
        *rest,
        half=0,
        deps=(near1_on,),
    )
    far1 = hand(a1_far, (sums[4],))
    far1_below, far1_above = both_ways(far1, 0, 1)
    far0_on = pick(core1, far0_below, far0_above, (far1,))
    far0_far = across(far0_on, 0, 1)
    sketch13 = plane_pass(
        (1, 2),
        (a1_above, a1_below),
        (near1_above, near1_far, near1_below),
        *rest,
        half=1,
        sums=sums,
        deps=(far0_on,),
    )
    far1_on = pick(core1, far1_below, far1_above, (sketch13,))
    far1_far = across(far1_on, 0, 1)
    sums = plane_pass(
        (2, 1), (a0_far,), (far0_above, far0_far, far0_below), *rest, half=0, deps=(far1_on,)
    )
    parts = plane_pass(
        (2, 1),
        (far1,),
        (far1_above, far1_far, far1_below),
        *rest,
        half=1,
        sums=sums,
        before=(sketch0, sketch13),
    )

    total = (parts[0] + move(parts[2], 2, 0, 0)) + (move(parts[1], 1, 0, 0) + move(parts[3], 3, 0, 0))
    total = (total + move(total, 0, 0, 2)) + (move(total, 0, 0, 1) + move(total, 0, 0, 3))
    swapped = move(total, 0, 1, 0)
    train_sum = jnp.where(first, total, swapped)
    test_sum = jnp.where(first, swapped, total)
    row = lax.dynamic_slice_in_dim(train_sum, (ex - z) % 4, 1, 0)
    products = jnp.sum(row * test_sum, axis=(1, 2)) * rates[0]
    products = lax.dynamic_slice_in_dim(jnp.concatenate([products, products]), (4 - z) % 4, 4, 0)
    block = products.reshape(1, 4)

    ckpt = lambda v, d: lax.ppermute(v, ("ckpt",), y_pairs(d))
    block = (block + ckpt(block, 2)) + (ckpt(block, 1) + ckpt(block, 3))
    line = lambda d0, d1: lax.ppermute(block, EVERY, z_pairs(d0, d1))
    r0, r1, r2, r3 = line(4, 1), line(2, -3), line(-2, 3), line(None, -1)
    half = jnp.where(first, (block + r0) + (r1 + r2), (r0 + r1) + (r2 + r3))
    return half + move(half, 0, 1, 0)


def solution(mesh):
    fine = Mesh(mesh.devices.reshape(8, 4, 2, 4), EVERY)
    rows = GROUP
    in_specs = (
        P("ckpt", rows, None),
        P("ckpt", rows, None),
        P("ckpt", rows, None),
        P("ckpt", rows, None),
        P("ckpt", None, rows),
        P("ckpt", None, rows),
        P("ckpt", None, rows),
        P("ckpt", rows, None),
        P(rows, None),
        P(),
        P("ckpt"),
    )
    out_specs = P("ex", None)
    return jax.shard_map(body, mesh=fine, in_specs=in_specs, out_specs=out_specs, check_vma=False)
```
